128 devices in a mesh: blk: 32 (over y, z_hi, x), dp: 4 (over z_lo, core).
Axes of the slice: x: 4, y: 4, z: 4 (z_hi: 2, z_lo: 2; z = z_hi * 2 + z_lo), core: 2. Of those that a mesh axis runs over, the one named last changes fastest.
Arguments:
- image_embed: bfloat16 [98304, 1152], P(('dp', 'blk')), parts along dimension 0, may hold values from -0.1875 to 0.1875
- text_embed: bfloat16 [98304, 1152], P(('dp', 'blk')), parts along dimension 0, may hold values from -0.1875 to 0.1875
- logit_scale: float32 [1], replicated, may hold values from 4 to 10
- logit_bias: float32 [1], replicated, may hold values from -4 to -1
Outputs:
- image_grad: float32 [98304, 1152], P(('dp', 'blk')), parts along dimension 0
- text_grad: float32 [98304, 1152], P(('dp', 'blk')), parts along dimension 0
The draws below stay inside these ranges and needn't reach their ends.
There are 4 independent parts, one for each index of `dp`. The reference program is written for one: setup_inputs(seed, part) draws one part's arguments, and reference() takes and returns one part's arrays. A program takes and returns all parts, laid end to end along the dimension named above; an argument that names none is the same for every part. Nothing has to cross between parts.
All inputs are finite; a program needn't handle non-finite values.
Results may differ from the reference program's by a relative error of at most 0.0045.
Values may be sent and summed in bfloat16 or wider, within the bound.
A program may use at most 64 MiB of HBM per device.

```python
import jax
import jax.numpy as jnp
from jax import lax

D = 1152
ROWS = 768
ROUNDS = 4
BATCH = 24576
N_BLK = 32


def shard_levels(own_key, shape, split, low, high):
    loudness, own = 1.0, jax.random.fold_in(own_key, 6)
    for position, shards_of in split:
        steps = jnp.exp(jax.random.uniform(jax.random.fold_in(own, position), (shards_of,), jnp.float32, low / len(split), high / len(split)))
        loudness = loudness * jnp.repeat(steps, shape[position] // shards_of).reshape([-1 if axis == position else 1 for axis in range(len(shape))])
    return loudness


def noise(stream_key, shape, scale, most, split=(), kind=jnp.bfloat16):
    array = jax.random.normal(stream_key, shape, jnp.float32) * scale
    if len(split) > 0:
        array = shard_levels(stream_key, shape, split, -0.22, 0.18) * array
    return jnp.clip(array, min=-most, max=most).astype(kind)


def setup_inputs(seed: int = 0, part: int = 0) -> dict:
    streams_of = jax.random.split(jax.random.key(seed), 5)
    own_keys = jax.random.split(jax.random.fold_in(streams_of[4], part), 5)
    return {
        "image_embed": noise(own_keys[0], (BATCH, D), D ** -0.5, 0.1875, ((0, 32),)),
        "text_embed": noise(own_keys[1], (BATCH, D), D ** -0.5, 0.1875, ((0, 32),)),
        "logit_scale": jnp.clip(jax.random.uniform(streams_of[2], (1,), jnp.float32, 4.0, 10.0), 4.0, 10.0),
        "logit_bias": jnp.clip(jax.random.uniform(streams_of[3], (1,), jnp.float32, -4.0, -1.0), -4.0, -1.0),
    }


epsilon = 1e-06

def normalize(raw):
    values = raw.astype(jnp.float32)
    inverse = lax.rsqrt(lax.optimization_barrier(jnp.sum(values * values, axis=1, keepdims=True)) + epsilon)
    return (values * inverse, inverse)

def pair_terms(image_low, text_low, temper, offset, positive):
    logits = temper * lax.dot_general(image_low, text_low, (((1,), (1,)), ((), ())), preferred_element_type=jnp.float32) + offset
    weights = (temper * (jax.nn.sigmoid(logits) - positive)).astype(jnp.bfloat16)
    image_term = jnp.dot(weights, text_low, preferred_element_type=jnp.float32)
    text_term = lax.dot_general(weights, image_low, (((0,), (0,)), ((), ())), preferred_element_type=jnp.float32)
    return (image_term, text_term)

def project_back(unit, inverse, grad_unit):
    return (grad_unit - unit * lax.optimization_barrier(jnp.sum(unit * grad_unit, axis=1, keepdims=True))) * inverse

def reference(image_embed, text_embed, logit_scale, logit_bias):
    temper = logit_scale[0]
    offset = logit_bias[0]
    unit_image, inv_image = normalize(image_embed)
    unit_text, inv_text = normalize(text_embed)
    image_blocks = unit_image.astype(jnp.bfloat16).reshape(N_BLK, ROWS, D)
    text_blocks = unit_text.astype(jnp.bfloat16).reshape(N_BLK, ROWS, D)
    image_sums = jnp.zeros((N_BLK, ROWS, D), jnp.float32)
    text_sums = jnp.zeros((N_BLK, ROWS, D), jnp.float32)
    for round_index in range(ROUNDS):
        partner = jnp.roll(text_blocks, round_index, axis=0)
        if round_index == 0:
            positive = jnp.eye(ROWS, dtype=jnp.float32)
        else:
            positive = jnp.zeros((ROWS, ROWS), jnp.float32)

        def block_terms(both):
            return pair_terms(both[0], both[1], temper, offset, positive)
        image_term, text_term = lax.map(block_terms, (image_blocks, partner))
        image_sums = image_sums + image_term
        text_sums = text_sums + jnp.roll(text_term, -round_index, axis=0)
    image_grad = project_back(unit_image, inv_image, image_sums.reshape(N_BLK * ROWS, D))
    text_grad = project_back(unit_text, inv_text, text_sums.reshape(N_BLK * ROWS, D))
    return (image_grad, text_grad)
```

```python
import functools

import jax
import jax.numpy as jnp
from jax import lax
from jax.experimental import pallas as pl
from jax.experimental.pallas import tpu as pltpu
from jax.sharding import PartitionSpec as P

MESH = pl.DeviceIdType.MESH
ROW = 4
PARTS = 3
BACK = 6

epsilon = 1e-06

OWN_A, OWN_B, LENT_A, LENT_B, FAR_B = range(5)

def tile_order():
    steps = []

    def add(a, i, b, t, await_=-1, done=0, piece=0):
        steps.append((a, i, b, t, await_, done, piece))

    for i in range(PARTS):
        for t in range(PARTS):
            add(OWN_A, i, OWN_B, t)
    for c in range(PARTS - 1):
        add(OWN_A, 0, LENT_B, c, await_=c)
        for i in range(1, PARTS):
            add(OWN_A, i, LENT_B, c)
        for b in (LENT_B, -1):
            for k in range(c):
                add(LENT_A, k, b, c)
            for k in range(c + 1):
                add(LENT_A, c, b, k)
    c = PARTS - 1
    first = True
    for k in range(c):
        add(LENT_A, c, LENT_B, k, await_=c if first else -1, done=1, piece=k)
        first = False
        add(LENT_A, k, LENT_B, c)
        add(LENT_A, k, -1, c, done=2, piece=k)
    for k in range(c):
        add(LENT_A, c, -1, k, done=4, piece=k)
    for i in range(PARTS):
        add(OWN_A, i, LENT_B, c)
    add(LENT_A, c, LENT_B, c, done=1, piece=c)
    add(LENT_A, c, -1, c, done=6, piece=c)
    return steps


def pick(step, values):
    total = jnp.int32(0)
    for k, v in enumerate(values):
        if v != 0:
            total = total + jnp.where(step == k, jnp.int32(v), jnp.int32(0))
    return total


def kernel(
    image_ref, text_ref, scale_ref, bias_ref, image_out, text_out,
    raw, inv, low, acc, give, got,
    load_sem, send_sem, recv_sem, back_send_sem, back_recv_sem, out_sem,
):
    rows, _ = image_ref.shape
    size = rows // PARTS
    back = rows // BACK
    blk = lax.axis_index("blk")
    core = lax.rem(lax.axis_index("dp"), 2)
    x = lax.rem(blk, ROW)
    line = lax.div(blk, ROW)
    n_lines = lax.axis_size("blk") // ROW
    place = x + core * (ROW - 1 - 2 * x)
    sign = 1 - 2 * core
    odd = lax.rem(place, 2)
    upper = lax.div(place, 2)

    def block_at(shift, column):
        return lax.rem(line + shift + n_lines, n_lines) * ROW + column

    peer = block_at(0, x + 1 - 2 * lax.rem(x, 2))
    lent_to = block_at(sign * upper, ROW - 1 - x)
    lent_by = block_at(sign * (upper - 1), ROW - 1 - x)
    far_to = block_at(sign, x)
    far_by = block_at(-sign, x)

    def on(block):
        return {"blk": block}

    barrier = pltpu.get_barrier_semaphore()
    for block in (peer, lent_to, lent_by):
        pl.semaphore_signal(barrier, inc=1, device_id=on(block), device_id_type=MESH)

    @pl.when(odd == 1)
    def _():
        for block in (far_to, far_by):
            pl.semaphore_signal(barrier, inc=1, device_id=on(block), device_id_type=MESH)

    def load(source, slot, c):
        part = pl.ds(c * size, size)
        return pltpu.make_async_copy(
            source.at[part], raw.at[slot, part], load_sem.at[slot, c]
        )

    for c in range(PARTS):
        load(image_ref, core, c).start()
        load(text_ref, 1 - core, c).start()

    def send(flow, c):
        part = pl.ds(c * size, size)
        slot, place_, block = (
            (OWN_A, LENT_A, peer),
            (OWN_B, LENT_B, lent_to),
            (OWN_B, FAR_B, far_to),
        )[flow]
        return pltpu.make_async_remote_copy(
            low.at[slot, part], low.at[place_, part],
            send_sem.at[flow, c], recv_sem.at[flow, c],
            device_id=on(block), device_id_type=MESH,
        )

    def give_back(flow, r):
        part = pl.ds(r * back, back)
        block = (peer, lent_by, far_by)[flow]
        return pltpu.make_async_remote_copy(
            give.at[flow, part], got.at[flow, part],
            back_send_sem.at[flow, r], back_recv_sem.at[flow, r],
            device_id=on(block), device_id_type=MESH,
        )

    for c in range(PARTS):
        load(image_ref, core, c).wait()
        load(text_ref, 1 - core, c).wait()

        def normalize(k, _):
            slot = lax.div(k, 4)
            part = pl.ds(c * size + lax.rem(k, 4) * (size // 4), size // 4)
            values = raw[slot, part].astype(jnp.float32)
            inverse = lax.rsqrt(jnp.sum(values * values, axis=1, keepdims=True) + epsilon)
            inv[slot, part] = inverse
            low[slot, part] = (values * inverse).astype(jnp.bfloat16)
            return 0

        lax.fori_loop(0, 8, normalize, 0)
        if c == 0:
            pl.semaphore_wait(barrier, 3 + 2 * odd)

        send(0, c).start()
        send(1, c).start()

        @pl.when(odd == 1)
        def _():
            send(2, c).start()

    def clear(k, _):
        part = pl.ds(k * 64, 64)
        for slot in range(5):
            acc[slot, part] = jnp.zeros((64, acc.shape[2]), jnp.float32)
        return 0

    lax.fori_loop(0, rows // 64, clear, 0)

    temper = scale_ref[0]
    offset = bias_ref[0]
    order = tile_order()
    columns = list(zip(*order))

    def flush(flow, slot, piece):
        for h in range(BACK // PARTS):
            r = piece * (BACK // PARTS) + h
            part = pl.ds(r * back, back)
            give[flow, part] = acc[slot, part].astype(jnp.bfloat16)
            give_back(flow, r).start()

    def tile(step, _):
        a = pick(step, columns[0])
        i = pick(step, columns[1]) * size
        b = pick(step, [v if v >= 0 else 0 for v in columns[2]])
        b = b + pick(step, [int(v < 0) for v in columns[2]]) * (OWN_B + (FAR_B - OWN_B) * odd)
        t = pick(step, columns[3]) * size
        awaited = pick(step, [v + 1 for v in columns[4]])
        done = pick(step, columns[5])
        piece = pick(step, columns[6])

        @pl.when(awaited > 0)
        def _():
            send(0, awaited - 1).wait_recv()
            send(1, awaited - 1).wait_recv()

            @pl.when(odd == 1)
            def _():
                send(2, awaited - 1).wait_recv()

        part_a = pl.ds(pl.multiple_of(i, size), size)
        part_b = pl.ds(pl.multiple_of(t, size), size)
        first = low[a, part_a]
        second = low[b, part_b]
        logits = lax.dot_general(
            first, second, (((1,), (1,)), ((), ())), preferred_element_type=jnp.float32
        )
        row = lax.broadcasted_iota(jnp.int32, (size, size), 0)
        column = lax.broadcasted_iota(jnp.int32, (size, size), 1)
        own = jnp.logical_and(a == OWN_A, jnp.logical_and(b == OWN_B, i == t))
        span = jnp.where(own, 0, 2 * size)
        positive = jnp.where(row - column == span, 1.0, 0.0)
        weights = (temper * (jax.nn.sigmoid(temper * logits + offset) - positive)).astype(
            jnp.bfloat16
        )
        acc[a, part_a] += jnp.dot(weights, second, preferred_element_type=jnp.float32)
        acc[b, part_b] += lax.dot_general(
            weights, first, (((0,), (0,)), ((), ())), preferred_element_type=jnp.float32
        )

        @pl.when(lax.rem(done, 2) == 1)
        def _():
            flush(1, LENT_B, piece)

        @pl.when(lax.rem(lax.div(done, 2), 2) == 1)
        def _():
            flush(0, LENT_A, piece)

        @pl.when(jnp.logical_and(done >= 4, odd == 1))
        def _():
            flush(2, FAR_B, piece)

        return 0

    lax.fori_loop(0, len(order), tile, 0)

    def finish(r, _):
        part = pl.ds(pl.multiple_of(r * back, back), back)
        give_back(0, r).wait_recv()
        give_back(1, r).wait_recv()
        acc[OWN_A, part] += got[0, part].astype(jnp.float32)
        acc[OWN_B, part] += got[1, part].astype(jnp.float32)

        @pl.when(odd == 1)
        def _():
            give_back(2, r).wait_recv()
            acc[OWN_B, part] += got[2, part].astype(jnp.float32)

        for slot in (0, 1):
            inverse = inv[slot, part]
            unit = raw[slot, part].astype(jnp.float32) * inverse
            grad = acc[slot, part]
            acc[slot, part] = (
                grad - unit * jnp.sum(unit * grad, axis=1, keepdims=True)
            ) * inverse
        store(image_out, core, r).start()
        store(text_out, 1 - core, r).start()
        return 0

    def store(target, slot, r):
        part = pl.ds(pl.multiple_of(r * back, back), back)
        return pltpu.make_async_copy(acc.at[slot, part], target.at[part], out_sem.at[slot, r])

    lax.fori_loop(0, BACK, finish, 0)

    for flow in range(3):
        def settle(flow=flow):
            for c in range(PARTS):
                send(flow, c).wait_send()
            for r in range(BACK):
                give_back(flow, r).wait_send()

        if flow < 2:
            settle()
        else:
            pl.when(odd == 1)(settle)
    for r in range(BACK):
        store(image_out, core, r).wait()
        store(text_out, 1 - core, r).wait()


def shards(image_embed, text_embed, logit_scale, logit_bias):
    rows, width = image_embed.shape
    stack = lambda n, kind: pltpu.VMEM((n, rows, width), kind)
    return pl.pallas_call(
        kernel,
        out_shape=[jax.ShapeDtypeStruct((rows, width), jnp.float32)] * 2,
        in_specs=[pl.BlockSpec(memory_space=pl.ANY)] * 2
        + [pl.BlockSpec(memory_space=pltpu.SMEM)] * 2,
        out_specs=[pl.BlockSpec(memory_space=pl.ANY)] * 2,
        scratch_shapes=[
            stack(2, jnp.bfloat16),
            pltpu.VMEM((2, rows, 1), jnp.float32),
            stack(5, jnp.bfloat16),
            stack(5, jnp.float32),
            stack(3, jnp.bfloat16),
            stack(3, jnp.bfloat16),
            pltpu.SemaphoreType.DMA((2, PARTS)),
            pltpu.SemaphoreType.DMA((3, PARTS)),
            pltpu.SemaphoreType.DMA((3, PARTS)),
            pltpu.SemaphoreType.DMA((3, BACK)),
            pltpu.SemaphoreType.DMA((3, BACK)),
            pltpu.SemaphoreType.DMA((2, BACK)),
        ],
        compiler_params=pltpu.CompilerParams(
            collective_id=0, has_side_effects=True, vmem_limit_bytes=60 * 1024 * 1024
        ),
        cost_estimate=pl.CostEstimate(
            flops=24 * rows * rows * width, bytes_accessed=12 * rows * width,
            transcendentals=4 * rows * rows,
        ),
        name="pair_gradients",
    )(image_embed, text_embed, logit_scale, logit_bias)


def solution(mesh):
    return jax.shard_map(
        shards,
        mesh=mesh,
        in_specs=(P(("dp", "blk"), None), P(("dp", "blk"), None), P(), P()),
        out_specs=(P(("dp", "blk"), None), P(("dp", "blk"), None)),
        check_vma=False,
    )
```

```python
import functools

import jax
import jax.numpy as jnp
from jax import lax
from jax.experimental import pallas as pl
from jax.experimental.pallas import tpu as pltpu
from jax.sharding import PartitionSpec as P

MESH = pl.DeviceIdType.MESH
ROW = 4
CUTS = ((0, 512), (512, 256))
PARTS = len(CUTS)
STEP = 256
BACK = 6

epsilon = 1e-06

LOWER = ([(0, 0), (2, 0), (0, 1)], [(1, 0), (2, 1)], [(1, 1)])
UPPER = ([(1, 0), (1, 1)], [(0, 0), (2, 0)], [(0, 1), (2, 1)])


def kernel(
    image_ref, text_ref, scale_ref, bias_ref, out,
    raw, inv, firsts, seconds, weights, give, got,
    load_sem, send_sem, recv_sem, back_send_sem, back_recv_sem,
):
    rows, _ = image_ref.shape
    back = rows // BACK
    blk = lax.axis_index("blk")
    core = lax.rem(lax.axis_index("dp"), 2)
    x = lax.rem(blk, ROW)
    line = lax.div(blk, ROW)
    n_lines = lax.axis_size("blk") // ROW
    place = x + core * (ROW - 1 - 2 * x)
    sign = 1 - 2 * core
    odd = lax.rem(place, 2)
    upper = lax.div(place, 2)

    def block_at(shift, column):
        return lax.rem(line + shift + n_lines, n_lines) * ROW + column

    peer = block_at(0, x + 1 - 2 * lax.rem(x, 2))
    lent_to = block_at(sign * upper, ROW - 1 - x)
    lent_by = block_at(sign * (upper - 1), ROW - 1 - x)
    far_to = block_at(sign, x)
    far_by = block_at(-sign, x)

    def on(block):
        return {"blk": block}

    barrier = pltpu.get_barrier_semaphore()
    for block in (peer, lent_to, lent_by):
        pl.semaphore_signal(barrier, inc=1, device_id=on(block), device_id_type=MESH)

    @pl.when(odd == 1)
    def _():
        for block in (far_to, far_by):
            pl.semaphore_signal(barrier, inc=1, device_id=on(block), device_id_type=MESH)

    def load(source, slot, c):
        part = pl.ds(*CUTS[c])
        return pltpu.make_async_copy(
            source.at[part], raw.at[slot, part], load_sem.at[slot, c]
        )

    for c in range(PARTS):
        load(image_ref, core, c).start()
        load(text_ref, 1 - core, c).start()

    def send(flow, c):
        start, count = CUTS[c]
        buffer, place_, block = (
            (firsts, 1, peer), (seconds, 1, lent_to), (seconds, 2, far_to)
        )[flow]
        return pltpu.make_async_remote_copy(
            buffer.at[pl.ds(start, count)], buffer.at[pl.ds(place_ * rows + start, count)],
            send_sem.at[flow, c], recv_sem.at[flow, c],
            device_id=on(block), device_id_type=MESH,
        )

    def give_back(flow, r):
        part = pl.ds(r * back, back)
        block = (peer, lent_by, far_by)[flow]
        return pltpu.make_async_remote_copy(
            give.at[flow, part], got.at[flow, part],
            back_send_sem.at[flow, r], back_recv_sem.at[flow, r],
            device_id=on(block), device_id_type=MESH,
        )

    def begin(ready, flow, c):
        if flow == 2:
            ready = jnp.logical_and(ready, odd == 1)
        pl.when(ready)(lambda: send(flow, c).start())

    def begin(ready, flow, c):
        if flow == 2:
            ready = jnp.logical_and(ready, odd == 1)
        pl.when(ready)(lambda: send(flow, c).start())

    for c, (start, count) in enumerate(CUTS):
        load(image_ref, core, c).wait()
        load(text_ref, 1 - core, c).wait()

        def normalize(k, _):
            part = pl.ds(pl.multiple_of(start + k * 64, 64), 64)
            for slot, buffer in enumerate((firsts, seconds)):
                values = raw[slot, part].astype(jnp.float32)
                inverse = lax.rsqrt(jnp.sum(values * values, axis=1, keepdims=True) + epsilon)
                inv[slot, part] = inverse
                buffer[part] = (values * inverse).astype(jnp.bfloat16)
            return 0

        lax.fori_loop(0, count // 64, normalize, 0)
        if c == 0:
            pl.semaphore_wait(barrier, 3 + 2 * odd)
        for half, plan in enumerate((LOWER, UPPER)):
            for flow, piece in plan[0]:
                if piece == c:
                    begin(upper == half, flow, piece)

    def gate(half, c):
        here = upper == half
        pl.when(here)(lambda: send(half, c).wait_send())
        for flow, piece in (LOWER, UPPER)[half][1 + c]:
            begin(here, flow, piece)

    temper = scale_ref[0]
    offset = bias_ref[0]

    def weigh(first, last, start, count, own=False):
        def step(k, _):
            part = pl.ds(pl.multiple_of(k * STEP, STEP), STEP)
            logits = lax.dot_general(
                firsts[part], seconds[pl.ds(start, count)], (((1,), (1,)), ((), ())),
                preferred_element_type=jnp.float32,
            )
            slope = jax.nn.sigmoid(temper * logits + offset)
            if own:
                row = lax.broadcasted_iota(jnp.int32, logits.shape, 0) + k * STEP
                column = lax.broadcasted_iota(jnp.int32, logits.shape, 1)
                slope = slope - jnp.where(row == column, 1.0, 0.0)
            weights[part, pl.ds(start, count)] = (temper * slope).astype(jnp.bfloat16)
            return 0

        lax.fori_loop(first, last, step, 0)

    def first_sum(base, k, start, count):
        part = pl.ds(pl.multiple_of(base + k * STEP, STEP), STEP)
        across = pl.ds(start, count)
        return jnp.dot(weights[part, across], seconds[across], preferred_element_type=jnp.float32)

    def second_sum(base, k, start, count):
        part = pl.ds(pl.multiple_of(base + k * STEP, STEP), STEP)
        down = pl.ds(start, count)
        return lax.dot_general(
            weights[down, part], firsts[down], (((0,), (0,)), ((), ())),
            preferred_element_type=jnp.float32,
        )

    def flush(flow, k):
        if flow == 0:
            first_at = pl.multiple_of(odd * rows, rows)
            total = first_sum(rows, k, first_at, 2 * rows)
        elif flow == 1:
            total = second_sum(rows, k, 0, 2 * rows)
        else:
            total = second_sum(2 * rows, k, rows, rows)
        give[flow, pl.ds(pl.multiple_of(k * STEP, STEP), STEP)] = total.astype(jnp.bfloat16)
        for h in range(STEP // back):
            give_back(flow, k * (STEP // back) + h).start()

    blocks = rows // STEP
    whole = CUTS[0][1] // STEP
    weigh(0, blocks, 0, rows, own=True)
    gate(0, 0)
    gate(1, 0)
    gate(1, 1)
    send(1, 0).wait_recv()
    weigh(0, blocks, rows, CUTS[0][1])
    gate(0, 1)
    send(0, 0).wait_recv()
    weigh(blocks, blocks + whole, rows, CUTS[0][1])
    pl.when(odd == 0)(lambda: weigh(blocks, blocks + whole, 0, rows))
    send(0, 1).wait_recv()
    weigh(blocks + whole, 2 * blocks, rows, CUTS[0][1])
    pl.when(odd == 0)(lambda: weigh(blocks + whole, 2 * blocks, 0, rows))
    flush(1, 0)
    send(1, 1).wait_recv()
    weigh(blocks, 2 * blocks, rows + CUTS[1][0], CUTS[1][1])
    pl.when(odd == 0)(lambda: flush(0, 0))
    flush(1, 1)
    pl.when(odd == 0)(lambda: flush(0, 1))
    weigh(0, blocks, rows + CUTS[1][0], CUTS[1][1])
    flush(1, 2)
    pl.when(odd == 0)(lambda: flush(0, 2))

    @pl.when(odd == 1)
    def _():
        for c in range(PARTS):
            send(2, c).wait_recv()
        weigh(blocks, 2 * blocks, 2 * rows, rows)

        def both(k, _):
            flush(0, k)
            flush(2, k)
            return 0

        lax.fori_loop(0, blocks, both, 0)

    def own_sums(k, _):
        part = pl.ds(pl.multiple_of(k * STEP, STEP), STEP)
        out[0, part] = first_sum(0, k, 0, 2 * rows)

        @pl.when(odd == 0)
        def _():
            out[1, part] = second_sum(0, k, 0, 2 * rows)

        @pl.when(odd == 1)
        def _():
            out[1, part] = second_sum(0, k, 0, rows)

        return 0

    lax.fori_loop(0, blocks, own_sums, 0)

    def finish(r, _):
        part = pl.ds(pl.multiple_of(r * back, back), back)
        give_back(0, r).wait_recv()
        give_back(1, r).wait_recv()
        out[0, part] += got[0, part].astype(jnp.float32)
        out[1, part] += got[1, part].astype(jnp.float32)

        @pl.when(odd == 1)
        def _():
            give_back(2, r).wait_recv()
            out[1, part] += got[2, part].astype(jnp.float32)

        for slot in (0, 1):
            inverse = inv[slot, part]
            unit = raw[slot, part].astype(jnp.float32) * inverse
            grad = out[slot, part]
            out[slot, part] = (
                grad - unit * jnp.sum(unit * grad, axis=1, keepdims=True)
            ) * inverse
        return 0

    lax.fori_loop(0, BACK, finish, 0)

    for c in range(PARTS):
        pl.when(upper == 0)(lambda c=c: send(1, c).wait_send())
        pl.when(upper == 1)(lambda c=c: send(0, c).wait_send())
        pl.when(odd == 1)(lambda c=c: send(2, c).wait_send())
    for r in range(BACK):
        give_back(0, r).wait_send()
        give_back(1, r).wait_send()
        pl.when(odd == 1)(lambda r=r: give_back(2, r).wait_send())


def write_out(sums, image_out, text_out, sem):
    core = lax.rem(lax.axis_index("dp"), 2)
    copies = [
        pltpu.make_async_copy(sums.at[core], image_out, sem.at[0]),
        pltpu.make_async_copy(sums.at[1 - core], text_out, sem.at[1]),
    ]
    for copy in copies:
        copy.start()
    for copy in copies:
        copy.wait()


def shards(image_embed, text_embed, logit_scale, logit_bias):
    rows, width = image_embed.shape
    stack = lambda n, kind: pltpu.VMEM((n, rows, width), kind)
    result = jax.ShapeDtypeStruct((rows, width), jnp.float32)
    sums = pl.pallas_call(
        kernel,
        out_shape=pltpu.VMEM((2, rows, width), jnp.float32),
        in_specs=[pl.BlockSpec(memory_space=pl.ANY)] * 2
        + [pl.BlockSpec(memory_space=pltpu.SMEM)] * 2,
        out_specs=pl.BlockSpec(memory_space=pltpu.VMEM),
        scratch_shapes=[
            stack(2, jnp.bfloat16),
            pltpu.VMEM((2, rows, 1), jnp.float32),
            pltpu.VMEM((2 * rows, width), jnp.bfloat16),
            pltpu.VMEM((3 * rows, width), jnp.bfloat16),
            pltpu.VMEM((2 * rows, 3 * rows), jnp.bfloat16),
            stack(3, jnp.bfloat16),
            stack(3, jnp.bfloat16),
            pltpu.SemaphoreType.DMA((2, PARTS)),
            pltpu.SemaphoreType.DMA((3, PARTS)),
            pltpu.SemaphoreType.DMA((3, PARTS)),
            pltpu.SemaphoreType.DMA((3, BACK)),
            pltpu.SemaphoreType.DMA((3, BACK)),
        ],
        compiler_params=pltpu.CompilerParams(
            collective_id=0, has_side_effects=True, vmem_limit_bytes=50 * 1024 * 1024
        ),
        cost_estimate=pl.CostEstimate(
            flops=24 * rows * rows * width, bytes_accessed=12 * rows * width,
            transcendentals=4 * rows * rows,
        ),
        name="pair_gradients",
    )(image_embed, text_embed, logit_scale, logit_bias)
    return tuple(
        pl.pallas_call(
            write_out,
            out_shape=[result] * 2,
            in_specs=[pl.BlockSpec(memory_space=pltpu.VMEM)],
            out_specs=[pl.BlockSpec(memory_space=pl.ANY)] * 2,
            scratch_shapes=[pltpu.SemaphoreType.DMA((2,))],
            cost_estimate=pl.CostEstimate(
                flops=0, bytes_accessed=16 * rows * width, transcendentals=0
            ),
            compiler_params=pltpu.CompilerParams(vmem_limit_bytes=8 * 1024 * 1024),
            name="write_out",
        )(pltpu.with_memory_space_constraint(sums, pltpu.VMEM))
    )


def solution(mesh):
    return jax.shard_map(
        shards,
        mesh=mesh,
        in_specs=(P(("dp", "blk"), None), P(("dp", "blk"), None), P(), P()),
        out_specs=(P(("dp", "blk"), None), P(("dp", "blk"), None)),
        check_vma=False,
    )
```

```python
import functools

import jax
import jax.numpy as jnp
from jax import lax
from jax.experimental import pallas as pl
from jax.experimental.pallas import tpu as pltpu
from jax.sharding import PartitionSpec as P

MESH = pl.DeviceIdType.MESH
ROW = 4
PARTS = 3
BACK = 6

epsilon = 1e-06

LOWER = (
    [(0, 0), (0, 1), (0, 2)], [], [(2, 0)], [(1, 0), (1, 1), (2, 1), (1, 2), (2, 2)],
)
UPPER = (
    [(1, 0), (1, 1), (1, 2)], [], [], [(0, 0), (2, 0), (0, 1), (2, 1), (0, 2), (2, 2)],
)


def kernel(
    image_ref, text_ref, scale_ref, bias_ref, out,
    raw, inv, firsts, seconds, weights, give, got,
    load_sem, send_sem, recv_sem, back_send_sem, back_recv_sem,
):
    rows, _ = image_ref.shape
    back = rows // BACK
    size = rows // PARTS
    blk = lax.axis_index("blk")
    core = lax.rem(lax.axis_index("dp"), 2)
    x = lax.rem(blk, ROW)
    line = lax.div(blk, ROW)
    n_lines = lax.axis_size("blk") // ROW
    place = x + core * (ROW - 1 - 2 * x)
    sign = 1 - 2 * core
    odd = lax.rem(place, 2)
    upper = lax.div(place, 2)

    def block_at(shift, column):
        return lax.rem(line + shift + n_lines, n_lines) * ROW + column

    peer = block_at(0, x + 1 - 2 * lax.rem(x, 2))
    lent_to = block_at(sign * upper, ROW - 1 - x)
    lent_by = block_at(sign * (upper - 1), ROW - 1 - x)
    far_to = block_at(sign, x)
    far_by = block_at(-sign, x)

    def on(block):
        return {"blk": block}

    barrier = pltpu.get_barrier_semaphore()
    for block in (peer, lent_to, lent_by):
        pl.semaphore_signal(barrier, inc=1, device_id=on(block), device_id_type=MESH)

    @pl.when(odd == 1)
    def _():
        for block in (far_to, far_by):
            pl.semaphore_signal(barrier, inc=1, device_id=on(block), device_id_type=MESH)

    def load(source, slot, c):
        part = pl.ds(c * size, size)
        return pltpu.make_async_copy(
            source.at[part], raw.at[slot, part], load_sem.at[slot, c]
        )

    for c in range(PARTS):
        load(image_ref, core, c).start()
        load(text_ref, 1 - core, c).start()

    def send(flow, c):
        start, count = c * size, size
        buffer, place_, block = (
            (firsts, 1, peer), (seconds, 1, lent_to), (seconds, 2, far_to)
        )[flow]
        return pltpu.make_async_remote_copy(
            buffer.at[pl.ds(start, count)], buffer.at[pl.ds(place_ * rows + start, count)],
            send_sem.at[flow, c], recv_sem.at[flow, c],
            device_id=on(block), device_id_type=MESH,
        )

    def give_back(flow, r):
        part = pl.ds(r * back, back)
        block = (peer, lent_by, far_by)[flow]
        return pltpu.make_async_remote_copy(
            give.at[flow, part], got.at[flow, part],
            back_send_sem.at[flow, r], back_recv_sem.at[flow, r],
            device_id=on(block), device_id_type=MESH,
        )

    def begin(ready, flow, c):
        if flow == 2:
            ready = jnp.logical_and(ready, odd == 1)
        pl.when(ready)(lambda: send(flow, c).start())

    def begin(ready, flow, c):
        if flow == 2:
            ready = jnp.logical_and(ready, odd == 1)
        pl.when(ready)(lambda: send(flow, c).start())

    for c in range(PARTS):
        start, count = c * size, size
        load(image_ref, core, c).wait()
        load(text_ref, 1 - core, c).wait()

        def normalize(k, _):
            part = pl.ds(pl.multiple_of(start + k * 64, 64), 64)
            for slot, buffer in enumerate((firsts, seconds)):
                values = raw[slot, part].astype(jnp.float32)
                inverse = lax.rsqrt(jnp.sum(values * values, axis=1, keepdims=True) + epsilon)
                inv[slot, part] = inverse
                buffer[part] = (values * inverse).astype(jnp.bfloat16)
            return 0

        lax.fori_loop(0, count // 64, normalize, 0)
        if c == 0:
            pl.semaphore_wait(barrier, 3 + 2 * odd)
        for half, plan in enumerate((LOWER, UPPER)):
            for flow, piece in plan[0]:
                if piece == c:
                    begin(upper == half, flow, piece)

    def gate(half, c):
        here = upper == half
        pl.when(here)(lambda: send(half, c).wait_send())
        for flow, piece in (LOWER, UPPER)[half][1 + c]:
            begin(here, flow, piece)

    temper = scale_ref[0]
    offset = bias_ref[0]

    def weigh(first, last, start, count, own=False):
        def step(k, _):
            part = pl.ds(pl.multiple_of(k * size, size), size)
            logits = lax.dot_general(
                firsts[part], seconds[pl.ds(start, count)], (((1,), (1,)), ((), ())),
                preferred_element_type=jnp.float32,
            )
            slope = jax.nn.sigmoid(temper * logits + offset)
            if own:
                row = lax.broadcasted_iota(jnp.int32, logits.shape, 0) + k * size
                column = lax.broadcasted_iota(jnp.int32, logits.shape, 1)
                slope = slope - jnp.where(row == column, 1.0, 0.0)
            weights[part, pl.ds(start, count)] = (temper * slope).astype(jnp.bfloat16)
            return 0

        lax.fori_loop(first, last, step, 0)

    def first_sum(base, k, start, count):
        part = pl.ds(pl.multiple_of(base + k * size, size), size)
        across = pl.ds(start, count)
        return jnp.dot(weights[part, across], seconds[across], preferred_element_type=jnp.float32)

    def second_sum(base, k, start, count):
        part = pl.ds(pl.multiple_of(base + k * size, size), size)
        down = pl.ds(start, count)
        return lax.dot_general(
            weights[down, part], firsts[down], (((0,), (0,)), ((), ())),
            preferred_element_type=jnp.float32,
        )

    def form(flow, k):
        if flow == 0:
            first_at = pl.multiple_of(odd * rows, rows)
            total = first_sum(rows, k, first_at, 2 * rows)
        elif flow == 1:
            total = second_sum(rows, k, 0, 2 * rows)
        else:
            total = second_sum(2 * rows, k, rows, rows)
        give[flow, pl.ds(pl.multiple_of(k * size, size), size)] = total.astype(jnp.bfloat16)

    def launch(flow, k):
        for h in range(BACK // PARTS):
            give_back(flow, k * (BACK // PARTS) + h).start()

    def early(flow, k):
        form(flow, k)
        pl.when(upper == 1)(lambda: launch(flow, k))

    def if_even(action):
        pl.when(odd == 0)(action)

    weigh(0, PARTS, 0, rows, own=True)
    for c in range(PARTS):
        gate(0, c)
        gate(1, c)
    last = PARTS - 1
    for c in range(last):
        send(1, c).wait_recv()
        weigh(0, PARTS, rows + c * size, size)
        send(0, c).wait_recv()
        if_even(lambda: weigh(PARTS + c, PARTS + c + 1, 0, rows))
        weigh(PARTS + c, PARTS + c + 1, rows, (c + 1) * size)
        if c > 0:
            weigh(PARTS, PARTS + c, rows + c * size, size)
    send(1, last).wait_recv()
    weigh(PARTS, PARTS + last, rows + last * size, size)
    if_even(lambda: early(0, 0))
    send(0, last).wait_recv()
    weigh(PARTS + last, PARTS + last + 1, rows, rows)
    early(1, 0)
    if_even(lambda: early(0, 1))
    early(1, 1)
    if_even(lambda: weigh(PARTS + last, PARTS + last + 1, 0, rows))
    if_even(lambda: early(0, last))
    weigh(0, PARTS, rows + last * size, size)
    early(1, last)

    def weigh_far(c):
        send(2, c).wait_recv()
        weigh(PARTS, 2 * PARTS, 2 * rows + c * size, size)

    @pl.when(odd == 1)
    def _():
        for c in range(last):
            weigh_far(c)

    @pl.when(upper == 0)
    def _():
        for k in range(PARTS):
            launch(1, k)
            if_even(lambda k=k: launch(0, k))

    @pl.when(odd == 1)
    def _():
        weigh_far(last)

        def both(k, _):
            form(0, k)
            launch(0, k)
            form(2, k)
            launch(2, k)
            return 0

        lax.fori_loop(0, PARTS, both, 0)

    def own_sums(k, _):
        part = pl.ds(pl.multiple_of(k * size, size), size)
        out[0, part] = first_sum(0, k, 0, 2 * rows)

        @pl.when(odd == 0)
        def _():
            out[1, part] = second_sum(0, k, 0, 2 * rows)

        @pl.when(odd == 1)
        def _():
            out[1, part] = second_sum(0, k, 0, rows)

        return 0

    lax.fori_loop(0, PARTS, own_sums, 0)

    def finish(r, _):
        part = pl.ds(pl.multiple_of(r * back, back), back)
        give_back(0, r).wait_recv()
        give_back(1, r).wait_recv()
        out[0, part] += got[0, part].astype(jnp.float32)
        out[1, part] += got[1, part].astype(jnp.float32)

        @pl.when(odd == 1)
        def _():
            give_back(2, r).wait_recv()
            out[1, part] += got[2, part].astype(jnp.float32)

        for slot in (0, 1):
            inverse = inv[slot, part]
            unit = raw[slot, part].astype(jnp.float32) * inverse
            grad = out[slot, part]
            out[slot, part] = (
                grad - unit * jnp.sum(unit * grad, axis=1, keepdims=True)
            ) * inverse
        return 0

    lax.fori_loop(0, BACK, finish, 0)

    for c in range(PARTS):
        pl.when(upper == 1)(lambda c=c: send(0, c).wait_send())
        pl.when(upper == 0)(lambda c=c: send(1, c).wait_send())
        pl.when(odd == 1)(lambda c=c: send(2, c).wait_send())
    for r in range(BACK):
        give_back(0, r).wait_send()
        give_back(1, r).wait_send()
        pl.when(odd == 1)(lambda r=r: give_back(2, r).wait_send())


def write_out(sums, image_out, text_out, sem):
    core = lax.rem(lax.axis_index("dp"), 2)
    copies = [
        pltpu.make_async_copy(sums.at[core], image_out, sem.at[0]),
        pltpu.make_async_copy(sums.at[1 - core], text_out, sem.at[1]),
    ]
    for copy in copies:
        copy.start()
    for copy in copies:
        copy.wait()


def shards(image_embed, text_embed, logit_scale, logit_bias):
    rows, width = image_embed.shape
    stack = lambda n, kind: pltpu.VMEM((n, rows, width), kind)
    result = jax.ShapeDtypeStruct((rows, width), jnp.float32)
    sums = pl.pallas_call(
        kernel,
        out_shape=pltpu.VMEM((2, rows, width), jnp.float32),
        in_specs=[pl.BlockSpec(memory_space=pl.ANY)] * 2
        + [pl.BlockSpec(memory_space=pltpu.SMEM)] * 2,
        out_specs=pl.BlockSpec(memory_space=pltpu.VMEM),
        scratch_shapes=[
            stack(2, jnp.bfloat16),
            pltpu.VMEM((2, rows, 1), jnp.float32),
            pltpu.VMEM((2 * rows, width), jnp.bfloat16),
            pltpu.VMEM((3 * rows, width), jnp.bfloat16),
            pltpu.VMEM((2 * rows, 3 * rows), jnp.bfloat16),
            stack(3, jnp.bfloat16),
            stack(3, jnp.bfloat16),
            pltpu.SemaphoreType.DMA((2, PARTS)),
            pltpu.SemaphoreType.DMA((3, PARTS)),
            pltpu.SemaphoreType.DMA((3, PARTS)),
            pltpu.SemaphoreType.DMA((3, BACK)),
            pltpu.SemaphoreType.DMA((3, BACK)),
        ],
        compiler_params=pltpu.CompilerParams(
            collective_id=0, has_side_effects=True, vmem_limit_bytes=50 * 1024 * 1024
        ),
        cost_estimate=pl.CostEstimate(
            flops=24 * rows * rows * width, bytes_accessed=12 * rows * width,
            transcendentals=4 * rows * rows,
        ),
        name="pair_gradients",
    )(image_embed, text_embed, logit_scale, logit_bias)
    return tuple(
        pl.pallas_call(
            write_out,
            out_shape=[result] * 2,
            in_specs=[pl.BlockSpec(memory_space=pltpu.VMEM)],
            out_specs=[pl.BlockSpec(memory_space=pl.ANY)] * 2,
            scratch_shapes=[pltpu.SemaphoreType.DMA((2,))],
            cost_estimate=pl.CostEstimate(
                flops=0, bytes_accessed=16 * rows * width, transcendentals=0
            ),
            compiler_params=pltpu.CompilerParams(vmem_limit_bytes=8 * 1024 * 1024),
            name="write_out",
        )(pltpu.with_memory_space_constraint(sums, pltpu.VMEM))
    )


def solution(mesh):
    return jax.shard_map(
        shards,
        mesh=mesh,
        in_specs=(P(("dp", "blk"), None), P(("dp", "blk"), None), P(), P()),
        out_specs=(P(("dp", "blk"), None), P(("dp", "blk"), None)),
        check_vma=False,
    )
```

```python
import functools

import jax
import jax.numpy as jnp
from jax import lax
from jax.experimental import pallas as pl
from jax.experimental.pallas import tpu as pltpu
from jax.sharding import PartitionSpec as P

MESH = pl.DeviceIdType.MESH
ROW = 4
PARTS = 3
BACK = 6

epsilon = 1e-06

LOWER = (
    [(0, 0), (0, 1), (0, 2)], [], [(2, 0)], [(1, 0), (1, 1), (2, 1), (1, 2), (2, 2)],
)
UPPER = (
    [(1, 0), (1, 1), (1, 2)], [], [], [(0, 0), (2, 0), (0, 1), (2, 1), (0, 2), (2, 2)],
)


def kernel(
    image_ref, text_ref, scale_ref, bias_ref, out,
    raw, inv, firsts, seconds, weights, give, got,
    load_sem, send_sem, recv_sem, back_send_sem, back_recv_sem,
):
    rows, _ = image_ref.shape
    back = rows // BACK
    size = rows // PARTS
    blk = lax.axis_index("blk")
    core = lax.rem(lax.axis_index("dp"), 2)
    x = lax.rem(blk, ROW)
    line = lax.div(blk, ROW)
    n_lines = lax.axis_size("blk") // ROW
    place = x + core * (ROW - 1 - 2 * x)
    sign = 1 - 2 * core
    odd = lax.rem(place, 2)
    upper = lax.div(place, 2)

    def block_at(shift, column):
        return lax.rem(line + shift + n_lines, n_lines) * ROW + column

    peer = block_at(0, x + 1 - 2 * lax.rem(x, 2))
    lent_to = block_at(sign * upper, ROW - 1 - x)
    lent_by = block_at(sign * (upper - 1), ROW - 1 - x)
    far_to = block_at(sign, x)
    far_by = block_at(-sign, x)

    def on(block):
        return {"blk": block}

    barrier = pltpu.get_barrier_semaphore()
    for block in (peer, lent_to, lent_by):
        pl.semaphore_signal(barrier, inc=1, device_id=on(block), device_id_type=MESH)

    @pl.when(odd == 1)
    def _():
        for block in (far_to, far_by):
            pl.semaphore_signal(barrier, inc=1, device_id=on(block), device_id_type=MESH)

    def load(source, slot, c):
        part = pl.ds(c * size, size)
        return pltpu.make_async_copy(
            source.at[part], raw.at[slot, part], load_sem.at[slot, c]
        )

    for c in range(PARTS):
        load(image_ref, core, c).start()
        load(text_ref, 1 - core, c).start()

    def send(flow, c):
        start, count = c * size, size
        buffer, place_, block = (
            (firsts, 1, peer), (seconds, 1, lent_to), (seconds, 2, far_to)
        )[flow]
        return pltpu.make_async_remote_copy(
            buffer.at[pl.ds(start, count)], buffer.at[pl.ds(place_ * rows + start, count)],
            send_sem.at[flow, c], recv_sem.at[flow, c],
            device_id=on(block), device_id_type=MESH,
        )

    def give_back(flow, r):
        part = pl.ds(r * back, back)
        block = (peer, lent_by, far_by)[flow]
        return pltpu.make_async_remote_copy(
            give.at[flow, part], got.at[flow, part],
            back_send_sem.at[flow, r], back_recv_sem.at[flow, r],
            device_id=on(block), device_id_type=MESH,
        )

    def begin(ready, flow, c):
        if flow == 2:
            ready = jnp.logical_and(ready, odd == 1)
        pl.when(ready)(lambda: send(flow, c).start())

    def begin(ready, flow, c):
        if flow == 2:
            ready = jnp.logical_and(ready, odd == 1)
        pl.when(ready)(lambda: send(flow, c).start())

    for c in range(PARTS):
        start, count = c * size, size
        load(image_ref, core, c).wait()
        load(text_ref, 1 - core, c).wait()

        def normalize(k, _):
            part = pl.ds(pl.multiple_of(start + k * 64, 64), 64)
            for slot, buffer in enumerate((firsts, seconds)):
                values = raw[slot, part].astype(jnp.float32)
                inverse = lax.rsqrt(jnp.sum(values * values, axis=1, keepdims=True) + epsilon)
                inv[slot, part] = inverse
                buffer[part] = (values * inverse).astype(jnp.bfloat16)
            return 0

        lax.fori_loop(0, count // 64, normalize, 0)
        if c == 0:
            pl.semaphore_wait(barrier, 3 + 2 * odd)
        for half, plan in enumerate((LOWER, UPPER)):
            for flow, piece in plan[0]:
                if piece == c:
                    begin(upper == half, flow, piece)

    def gate(half, c):
        here = upper == half
        pl.when(here)(lambda: send(half, c).wait_send())
        for flow, piece in (LOWER, UPPER)[half][1 + c]:
            begin(here, flow, piece)

    temper = scale_ref[0]
    offset = bias_ref[0]

    def weigh(first, last, start, count, own=False):
        def step(k, _):
            part = pl.ds(pl.multiple_of(k * size, size), size)
            logits = lax.dot_general(
                firsts[part], seconds[pl.ds(start, count)], (((1,), (1,)), ((), ())),
                preferred_element_type=jnp.float32,
            )
            slope = jax.nn.sigmoid(temper * logits + offset)
            if own:
                row = lax.broadcasted_iota(jnp.int32, logits.shape, 0) + k * size
                column = lax.broadcasted_iota(jnp.int32, logits.shape, 1)
                slope = slope - jnp.where(row == column, 1.0, 0.0)
            weights[part, pl.ds(start, count)] = (temper * slope).astype(jnp.bfloat16)
            return 0

        lax.fori_loop(first, last, step, 0)

    def first_sum(base, k, start, count):
        part = pl.ds(pl.multiple_of(base + k * size, size), size)
        across = pl.ds(start, count)
        return jnp.dot(weights[part, across], seconds[across], preferred_element_type=jnp.float32)

    def second_sum(base, k, start, count):
        part = pl.ds(pl.multiple_of(base + k * size, size), size)
        down = pl.ds(start, count)
        return lax.dot_general(
            weights[down, part], firsts[down], (((0,), (0,)), ((), ())),
            preferred_element_type=jnp.float32,
        )

    def form(flow, k):
        if flow == 0:
            first_at = pl.multiple_of(odd * rows, rows)
            total = first_sum(rows, k, first_at, 2 * rows)
        elif flow == 1:
            total = second_sum(rows, k, 0, 2 * rows)
        else:
            total = second_sum(2 * rows, k, rows, rows)
        give[flow, pl.ds(pl.multiple_of(k * size, size), size)] = total.astype(jnp.bfloat16)

    def launch(flow, k):
        for h in range(BACK // PARTS):
            give_back(flow, k * (BACK // PARTS) + h).start()

    def early(flow, k):
        form(flow, k)
        pl.when(upper == 1)(lambda: launch(flow, k))

    def if_even(action):
        pl.when(odd == 0)(action)

    weigh(0, PARTS, 0, rows, own=True)
    for c in range(PARTS):
        gate(0, c)
        gate(1, c)
    last = PARTS - 1
    for c in range(last):
        send(1, c).wait_recv()
        weigh(0, PARTS, rows + c * size, size)
        send(0, c).wait_recv()
        if_even(lambda: weigh(PARTS + c, PARTS + c + 1, 0, rows))
        weigh(PARTS + c, PARTS + c + 1, rows, (c + 1) * size)
        if c > 0:
            weigh(PARTS, PARTS + c, rows + c * size, size)
    send(1, last).wait_recv()
    weigh(PARTS, PARTS + last, rows + last * size, size)
    if_even(lambda: early(0, 0))
    send(0, last).wait_recv()
    weigh(PARTS + last, PARTS + last + 1, rows, rows)
    early(1, 0)
    if_even(lambda: early(0, 1))
    early(1, 1)
    if_even(lambda: weigh(PARTS + last, PARTS + last + 1, 0, rows))
    if_even(lambda: early(0, last))
    weigh(0, PARTS, rows + last * size, size)
    early(1, last)

    def weigh_far(c):
        send(2, c).wait_recv()
        weigh(PARTS, 2 * PARTS, 2 * rows + c * size, size)

    @pl.when(odd == 1)
    def _():
        for c in range(last):
            weigh_far(c)

    @pl.when(upper == 0)
    def _():
        for k in range(PARTS):
            launch(1, k)
            if_even(lambda k=k: launch(0, k))

    @pl.when(odd == 1)
    def _():
        weigh_far(last)

        def both(k, _):
            form(2, k)
            launch(2, k)
            form(0, k)
            launch(0, k)
            return 0

        lax.fori_loop(0, PARTS, both, 0)

    def own_sums(k, _):
        part = pl.ds(pl.multiple_of(k * size, size), size)
        out[0, part] = first_sum(0, k, 0, 2 * rows)

        @pl.when(odd == 0)
        def _():
            out[1, part] = second_sum(0, k, 0, 2 * rows)

        @pl.when(odd == 1)
        def _():
            out[1, part] = second_sum(0, k, 0, rows)

        return 0

    lax.fori_loop(0, PARTS, own_sums, 0)

    def finish(r, _):
        part = pl.ds(pl.multiple_of(r * back, back), back)
        give_back(0, r).wait_recv()
        give_back(1, r).wait_recv()
        out[0, part] += got[0, part].astype(jnp.float32)
        out[1, part] += got[1, part].astype(jnp.float32)

        @pl.when(odd == 1)
        def _():
            give_back(2, r).wait_recv()
            out[1, part] += got[2, part].astype(jnp.float32)

        for slot in (0, 1):
            inverse = inv[slot, part]
            unit = raw[slot, part].astype(jnp.float32) * inverse
            grad = out[slot, part]
            out[slot, part] = (
                grad - unit * jnp.sum(unit * grad, axis=1, keepdims=True)
            ) * inverse
        return 0

    lax.fori_loop(0, BACK, finish, 0)

    for c in range(PARTS):
        pl.when(upper == 1)(lambda c=c: send(0, c).wait_send())
        pl.when(upper == 0)(lambda c=c: send(1, c).wait_send())
        pl.when(odd == 1)(lambda c=c: send(2, c).wait_send())
    for r in range(BACK):
        give_back(0, r).wait_send()
        give_back(1, r).wait_send()
        pl.when(odd == 1)(lambda r=r: give_back(2, r).wait_send())


def write_out(sums, image_out, text_out, sem):
    core = lax.rem(lax.axis_index("dp"), 2)
    copies = [
        pltpu.make_async_copy(sums.at[core], image_out, sem.at[0]),
        pltpu.make_async_copy(sums.at[1 - core], text_out, sem.at[1]),
    ]
    for copy in copies:
        copy.start()
    for copy in copies:
        copy.wait()


def shards(image_embed, text_embed, logit_scale, logit_bias):
    rows, width = image_embed.shape
    stack = lambda n, kind: pltpu.VMEM((n, rows, width), kind)
    result = jax.ShapeDtypeStruct((rows, width), jnp.float32)
    sums = pl.pallas_call(
        kernel,
        out_shape=pltpu.VMEM((2, rows, width), jnp.float32),
        in_specs=[pl.BlockSpec(memory_space=pl.ANY)] * 2
        + [pl.BlockSpec(memory_space=pltpu.SMEM)] * 2,
        out_specs=pl.BlockSpec(memory_space=pltpu.VMEM),
        scratch_shapes=[
            stack(2, jnp.bfloat16),
            pltpu.VMEM((2, rows, 1), jnp.float32),
            pltpu.VMEM((2 * rows, width), jnp.bfloat16),
            pltpu.VMEM((3 * rows, width), jnp.bfloat16),
            pltpu.VMEM((2 * rows, 3 * rows), jnp.bfloat16),
            stack(3, jnp.bfloat16),
            stack(3, jnp.bfloat16),
            pltpu.SemaphoreType.DMA((2, PARTS)),
            pltpu.SemaphoreType.DMA((3, PARTS)),
            pltpu.SemaphoreType.DMA((3, PARTS)),
            pltpu.SemaphoreType.DMA((3, BACK)),
            pltpu.SemaphoreType.DMA((3, BACK)),
        ],
        compiler_params=pltpu.CompilerParams(
            collective_id=0, has_side_effects=True, vmem_limit_bytes=50 * 1024 * 1024
        ),
        cost_estimate=pl.CostEstimate(
            flops=24 * rows * rows * width, bytes_accessed=12 * rows * width,
            transcendentals=4 * rows * rows,
        ),
        name="pair_gradients",
    )(image_embed, text_embed, logit_scale, logit_bias)
    return tuple(
        pl.pallas_call(
            write_out,
            out_shape=[result] * 2,
            in_specs=[pl.BlockSpec(memory_space=pltpu.VMEM)],
            out_specs=[pl.BlockSpec(memory_space=pl.ANY)] * 2,
            scratch_shapes=[pltpu.SemaphoreType.DMA((2,))],
            cost_estimate=pl.CostEstimate(
                flops=0, bytes_accessed=16 * rows * width, transcendentals=0
            ),
            compiler_params=pltpu.CompilerParams(vmem_limit_bytes=8 * 1024 * 1024),
            name="write_out",
        )(pltpu.with_memory_space_constraint(sums, pltpu.VMEM))
    )


def solution(mesh):
    return jax.shard_map(
        shards,
        mesh=mesh,
        in_specs=(P(("dp", "blk"), None), P(("dp", "blk"), None), P(), P()),
        out_specs=(P(("dp", "blk"), None), P(("dp", "blk"), None)),
        check_vma=False,
    )
```
